256 devices in a mesh: outer: 16 (over z, x_lo), inner: 16 (over x_hi, y, core).
Axes of the slice: x: 4 (x_hi: 2, x_lo: 2; x = x_hi * 2 + x_lo), y: 4, z: 8, core: 2. Of those that a mesh axis runs over, the one named last changes fastest.
Arguments:
- queries: bfloat16 [32768, 4096], P(('outer', 'inner')), may hold values from -64 to 64
- keys: bfloat16 [32768, 1024], P(('outer', 'inner')), may hold values from -8 to 8
- values: bfloat16 [32768, 1024], P(('outer', 'inner')), may hold values from -6 to 6
- span_order: int32 [512], replicated, may hold values from 0 to 511, as said below
Outputs:
- attended: bfloat16 [32768, 4096], P(('outer', 'inner'))
The draws below stay inside these ranges and needn't reach their ends.
Inputs may be any that keep to these rules, and one draw needn't show every extreme that they name: span_order is a permutation of 0 .. 511, and the two spans of every device sum to 511.
All inputs are finite; a program needn't handle non-finite values.
Results may differ from the reference program's by a relative error of at most 0.0055.
Values may be sent and summed in bfloat16 or wider, within the bound.
A program may use at most 64 MiB of HBM per device.

```python
import math
import jax
import jax.numpy as jnp
from jax import lax

QH = 32
KVH = 8
HEAD = 128
GROUP = 4
SPAN = 64
INNER_STEPS = 3
OUTER_ROUNDS = 2
NCHUNKS = 512
TOKENS = 32768
N_OUTER = 16
N_INNER = 16


def keys_from(key):
    first = jax.random.fold_in(key, 0)
    shape = (TOKENS, KVH * HEAD)
    base = jax.random.truncated_normal(first, -6.0, 6.0, shape, jnp.float32)
    row_index = jnp.arange(TOKENS, dtype=jnp.int32)[:, None]
    tied = row_index % (2 * SPAN) == SPAN // 2 - 1
    mixed_rows = base
    return jnp.where(tied, mixed_rows, base)


def draw_keys(key, part):
    shared = keys_from(key)
    return shared.astype(jnp.bfloat16)


def draw_queries(key, part):
    key = jax.random.fold_in(key, 3)
    first = jax.random.fold_in(key, 0)
    shape = (TOKENS, QH * HEAD)
    base = jax.random.truncated_normal(first, -6.0, 6.0, shape, jnp.float32)
    row_index = jnp.arange(TOKENS, dtype=jnp.int32)[:, None]
    chosen = row_index % (2 * SPAN) == SPAN // 2
    replaced = base
    return jnp.where(chosen, replaced, base).astype(jnp.bfloat16)


def draw_span_order(key, part):
    key = jax.random.fold_in(key, 5)
    first, second = jax.random.split(key)
    halves = NCHUNKS // 2
    order = jax.random.permutation(first, halves).astype(jnp.int32)
    flipped = jax.random.randint(second, (halves,), 0, 2, jnp.int32)
    early = jnp.where(flipped == 1, NCHUNKS - 1 - order, order)
    later = NCHUNKS - 1 - early
    return jnp.stack([early, later], axis=1).reshape(NCHUNKS).astype(jnp.int32)


def shard_levels(rng, dims, cuts, low, high):
    def one(position, shards_of):
        heights = jax.random.uniform(jax.random.fold_in(jax.random.fold_in(rng, 6), position), (shards_of,), jnp.float32, low / len(cuts), high / len(cuts))
        return jnp.repeat(jnp.exp(heights), dims[position] // shards_of).reshape((-1,) + (1,) * (len(dims) - position - 1))

    gain = one(*cuts[0])
    for cut in cuts[1:]:
        gain = gain * one(*cut)
    return gain


def gaussian(stream_key, extent, width, limit, cuts=(), kind=jnp.bfloat16):
    entries = width * jax.random.normal(stream_key, extent, jnp.float32)
    if cuts:
        entries = entries * shard_levels(stream_key, extent, cuts, -0.22, 0.18)
    return jnp.clip(entries, -limit, limit).astype(kind)


def setup_inputs(seed: int = 0) -> dict:
    seeds = jax.random.split(jax.random.key(seed), 5)
    return {
        "queries": draw_queries(jax.random.fold_in(seeds[4], 71), 0),
        "keys": draw_keys(jax.random.fold_in(seeds[4], 71), 0),
        "values": gaussian(seeds[2], (TOKENS, KVH * HEAD), 1.0, 6.0, ((0, 256),)),
        "span_order": draw_span_order(jax.random.fold_in(seeds[4], 71), 0),
    }


def token_positions(span_order, device, span_len):
    offsets = jnp.arange(2 * span_len, dtype=jnp.int32)
    starts = jnp.take(span_order, 2 * device + offsets // span_len)
    return starts * span_len + offsets % span_len

def reference(queries, keys, values, span_order):
    row_count = 2 * SPAN
    score_scale = 1.0 / math.sqrt(HEAD)

    def per_device(device):
        outer_id = device // N_INNER
        inner_id = device % N_INNER
        query_pos = token_positions(span_order, device, SPAN)
        query_rows = lax.dynamic_slice_in_dim(queries, device * row_count, row_count, 0)
        grouped = query_rows.astype(jnp.float32).reshape(row_count, KVH, GROUP, HEAD)
        key_list = []
        value_list = []
        pos_list = []
        for rounds in range(OUTER_ROUNDS):
            for rotation in range(INNER_STEPS + 1):
                source = (outer_id - rounds) % N_OUTER * N_INNER + (inner_id - rotation) % N_INNER
                source = source.astype(jnp.int32)
                key_list.append(lax.dynamic_slice_in_dim(keys, source * row_count, row_count, 0))
                value_list.append(lax.dynamic_slice_in_dim(values, source * row_count, row_count, 0))
                pos_list.append(token_positions(span_order, source, SPAN))
        all_keys = jnp.concatenate(key_list, 0).astype(jnp.float32).reshape(-1, KVH, HEAD)
        all_values = jnp.concatenate(value_list, 0).astype(jnp.float32).reshape(-1, KVH, HEAD)
        all_pos = jnp.concatenate(pos_list, 0)
        scores = jnp.einsum('tgrd,ugd->tgru', grouped, all_keys) * score_scale
        visible = all_pos[None, :] <= query_pos[:, None]
        scores = jnp.where(visible[:, None, None, :], scores, -jnp.inf)
        row_peak = lax.optimization_barrier(jnp.max(scores, axis=-1, keepdims=True))
        weights = jnp.exp(scores - row_peak)
        totals = lax.optimization_barrier(jnp.sum(weights, axis=-1))
        rounded = lax.optimization_barrier(weights.astype(jnp.bfloat16)).astype(jnp.float32)
        blended = jnp.einsum('tgru,ugd->tgrd', rounded, all_values) / totals[..., None]
        return blended.reshape(row_count, QH * HEAD).astype(jnp.bfloat16)
    result = lax.map(per_device, jnp.arange(N_OUTER * N_INNER, dtype=jnp.int32))
    return result.reshape(TOKENS, QH * HEAD)
```

```python
import functools
import math

import jax
import jax.numpy as jnp
from jax import lax
from jax.experimental import pallas as pl
from jax.experimental.pallas import tpu as pltpu
from jax.sharding import PartitionSpec as P

ROLES = 6
BLOCKS = 2
HEADS = 4
GROUP = 4
HEAD = 128
QUARTER = GROUP * HEAD
MESH = pl.DeviceIdType.MESH
MASKED = -1e30

OFFSETS = ((-1, 1), (-1, 2), (0, -1), (0, 1), (0, 2), (1, -1), (1, 0), (1, 1), (1, 2))

ORDER = (3, 2, 1, 5, 4)

ROUTES = {
    (0, 0, 1): (0xFF3F, 0x7F3F, 0x3F3F, 0x3F3F),
    (0, 0, 3): (0xFFFF, 0xFFFF, 0xFFFF, 0xFFFF),
    (0, 0, 4): (0x00C0, 0x80C0, 0xC0C0, 0xC8CB),
    (0, 1, 1): (0x3030, 0x3030, 0x3000, 0x1000),
    (0, 1, 2): (0xFF0F, 0xFF8F, 0xCFFF, 0xEFFF),
    (0, 1, 3): (0xFFFF, 0xFFFF, 0xFFFF, 0xFFFF),
    (0, 1, 4): (0x0000, 0x0080, 0x0000, 0x0000),
    (0, 1, 5): (0x00F0, 0x8070, 0xF800, 0xDC8C),
    (1, 0, 4): (0xCFDC, 0x05C4, 0x00C0, 0x0000),
    (2, 1, 1): (0xFCF0, 0xFCF8, 0xFCFF, 0xFEFF),
    (2, 1, 4): (0x0F00, 0x0700, 0x000F, 0x0207),
    (2, 1, 5): (0x3F30, 0x3738, 0x30FF, 0x3237),
    (3, 0, 1): (0xC000, 0xC080, 0xC0C0, 0xC0C0),
    (3, 0, 4): (0x080C, 0x0E3E, 0x0F3F, 0x3437),
    (3, 1, 1): (0xC000, 0x4000, 0x0000, 0x0000),
    (3, 1, 2): (0xF000, 0x7000, 0x0030, 0x0010),
    (3, 1, 4): (0x0F0F, 0x0F0F, 0x0F07, 0x0303),
    (3, 1, 5): (0x0C0C, 0x0C0C, 0x0004, 0x0000),
    (5, 1, 4): (0x0F00, 0x0708, 0x008F, 0xC8CD),
}

SEEN = {
    0: ((0,), (0, 1)),
    1: ((0, 1), (0, 1)),
    2: ((1,), ()),
    3: ((0,), (0, 1)),
    4: ((0, 1), (0, 1)),
    5: ((1,), ()),
}


def needed(role):
    return sorted(set(SEEN[role][0]) | set(SEEN[role][1]))


def kernel(order_ref, q_ref, k_ref, v_ref, o_ref, held, qbuf, obuf, peak, total, acc, hidden,
           send_sem, recv_sem, swap_sem, q_sem, qswap_sem, o_sem):
    n_outer = lax.axis_size("outer")
    n_chips = lax.axis_size("inner") // 2
    outer = lax.axis_index("outer")
    inner = lax.axis_index("inner")
    chip, core = inner // 2, inner % 2
    kind = ((outer % 2) * 4 + chip % 4) * 2 + core
    other = 1 - core

    def device(d_outer, d_chip):
        return (
            lax.rem(outer + d_outer + n_outer, n_outer),
            lax.rem(chip + d_chip + n_chips, n_chips) * 2 + core,
        )

    twin = (outer, chip * 2 + other)

    barrier = pltpu.get_barrier_semaphore()
    for d_outer, d_chip in OFFSETS:
        pl.semaphore_signal(barrier, 1, device_id=device(-d_outer, -d_chip), device_id_type=MESH)
    pl.semaphore_signal(barrier, 1, device_id=twin, device_id_type=MESH)

    def own_copy(ref, part, head):
        columns = pl.ds((core * HEADS + head) * HEAD, HEAD)
        return pltpu.make_async_copy(
            ref.at[:, columns], held.at[0, core, head, part], recv_sem.at[0, core, head]
        )

    def twin_copy(ref, part, head):
        columns = pl.ds((other * HEADS + head) * HEAD, HEAD)
        return pltpu.make_async_remote_copy(
            src_ref=ref.at[:, columns],
            dst_ref=held.at[0, core, head, part],
            send_sem=swap_sem.at[head, part],
            recv_sem=recv_sem.at[0, core, head],
            device_id=twin,
            device_id_type=MESH,
        )

    width = HEADS * QUARTER

    def own_queries():
        return pltpu.make_async_copy(
            q_ref.at[:, pl.ds(core * width, width)], qbuf.at[core], q_sem.at[core]
        )

    def twin_queries():
        return pltpu.make_async_remote_copy(
            src_ref=q_ref.at[:, pl.ds(other * width, width)],
            dst_ref=qbuf.at[core],
            send_sem=qswap_sem,
            recv_sem=q_sem.at[core],
            device_id=twin,
            device_id_type=MESH,
        )

    for head in range(HEADS):
        for part, ref in enumerate((k_ref, v_ref)):
            own_copy(ref, part, head).start()
    own_queries().start()

    def hidden_tile(role, query_core, key_core):
        d_outer, d_chip = role // 3, role % 3
        at_outer, at_inner = device(-d_outer, -d_chip)
        source = at_outer * (2 * n_chips) + (at_inner - core) + key_core
        mine = outer * (2 * n_chips) + chip * 2 + query_core
        row = lax.broadcasted_iota(jnp.int32, (HEAD, HEAD), 0)
        column = lax.broadcasted_iota(jnp.int32, (HEAD, HEAD), 1)
        half = HEAD // 2
        row_at = jnp.where(row < half, order_ref[2 * mine] * half, order_ref[2 * mine + 1] * half - half) + row
        column_at = (
            jnp.where(column < half, order_ref[2 * source] * half, order_ref[2 * source + 1] * half - half) + column
        )
        return jnp.where(column_at <= row_at, 0.0, MASKED)

    def pass_on(role, block, head, unit):
        for there in range(1, ROLES):
            masks = ROUTES.get((role, block, there))
            if masks is None:
                continue
            mask = jnp.int32(masks[0])
            for at in range(1, HEADS):
                mask = jnp.where(head == at, jnp.int32(masks[at]), mask)
            copy = pltpu.make_async_remote_copy(
                src_ref=held.at[role, block, head],
                dst_ref=held.at[there, block, head],
                send_sem=send_sem.at[role, block, head, there - 1],
                recv_sem=recv_sem.at[there, block, head],
                device_id=device(there // 3 - role // 3, there % 3 - role % 3),
                device_id_type=MESH,
            )

            @pl.when(lax.rem(lax.shift_right_logical(mask, kind), 2) == 1)
            def _():
                unit(copy)

    def arrive(role, block, head):
        chunk = held.at[role, block, head]
        pltpu.make_async_copy(chunk, chunk, recv_sem.at[role, block, head]).wait()

    def start(copy):
        copy.start()

    def finish(copy):
        copy.wait_send()

    pl.semaphore_wait(barrier, len(OFFSETS) + 1)

    for head in range(HEADS):
        for part, ref in enumerate((k_ref, v_ref)):
            twin_copy(ref, part, head).start()

    @pl.loop(0, HEADS)
    def _(head):
        arrive(0, core, head)
        for block in range(BLOCKS):
            @pl.when(core == block)
            def _():
                pass_on(0, block, head, start)

    twin_queries().start()

    @pl.loop(0, HEADS)
    def _(head):
        arrive(0, other, head)
        for block in range(BLOCKS):
            @pl.when(other == block)
            def _():
                pass_on(0, block, head, start)

    for role in range(ROLES):
        for query_core in range(2):
            for key_core in SEEN[role][query_core]:
                hidden[role, query_core, key_core] = hidden_tile(role, query_core, key_core)

    scale = math.log2(math.e) / math.sqrt(HEAD)

    def attend(role, head):
        for query_core in range(2):
            seen = SEEN[role][query_core]
            if not seen:
                continue
            queries = jnp.concatenate(
                [
                    qbuf[query_core, :, pl.ds(pl.multiple_of((head * GROUP + at) * HEAD, HEAD), HEAD)]
                    for at in range(GROUP)
                ],
                axis=0,
            )
            scores = []
            for key_core in seen:
                score = lax.dot_general(
                    queries,
                    held[role, key_core, head, 0],
                    (((1,), (1,)), ((), ())),
                    preferred_element_type=jnp.float32,
                )
                cover = hidden[role, query_core, key_core]
                score = score.reshape(GROUP, HEAD, HEAD) * scale + cover[None]
                scores.append(score.reshape(QUARTER, HEAD))
            top = scores[0] if len(seen) == 1 else jnp.maximum(scores[0], scores[1])
            top = jnp.max(top, axis=1, keepdims=True)
            if role == 0:
                new = jnp.broadcast_to(top, (QUARTER, HEAD))
            else:
                old = peak[query_core, head]
                new = jnp.maximum(old, top)
                factor = jnp.exp2(old - new)
            weights = [jnp.exp2(score - new) for score in scores]
            summed = weights[0] if len(seen) == 1 else weights[0] + weights[1]
            update = None
            for key_core, weight in zip(seen, weights):
                term = jnp.dot(
                    weight.astype(jnp.bfloat16),
                    held[role, key_core, head, 1],
                    preferred_element_type=jnp.float32,
                )
                update = term if update is None else update + term
            peak[query_core, head] = new
            if role == 0:
                total[query_core, head] = summed
                acc[query_core, head] = update
            else:
                total[query_core, head] = total[query_core, head] * factor + summed
                acc[query_core, head] = acc[query_core, head] * factor + update

    for query_core in range(2):
        pltpu.make_async_copy(qbuf.at[query_core], qbuf.at[query_core], q_sem.at[query_core]).wait()

    @pl.loop(0, HEADS)
    def _(head):
        attend(0, head)

    for role in ORDER:
        @pl.loop(0, HEADS)
        def _(head):
            for block in needed(role):
                arrive(role, block, head)
                pass_on(role, block, head, start)
            attend(role, head)

    def own_result(head):
        columns = pl.ds((core * HEADS + head) * QUARTER, QUARTER)
        return pltpu.make_async_copy(obuf.at[core, head], o_ref.at[:, columns], o_sem.at[0, head])

    def twin_result(head):
        columns = pl.ds((core * HEADS + head) * QUARTER, QUARTER)
        return pltpu.make_async_remote_copy(
            src_ref=obuf.at[other, head],
            dst_ref=o_ref.at[:, columns],
            send_sem=o_sem.at[1, head],
            recv_sem=o_sem.at[2, head],
            device_id=twin,
            device_id_type=MESH,
        )

    @pl.loop(0, HEADS)
    def _(head):
        for query_core in range(2):
            sums = jnp.sum(total[query_core, head], axis=1, keepdims=True)
            result = (acc[query_core, head] / sums).astype(jnp.bfloat16)
            for at in range(GROUP):
                obuf[query_core, head, :, at * HEAD : (at + 1) * HEAD] = result[at * HEAD : (at + 1) * HEAD]
        twin_result(head).start()
        own_result(head).start()

    for head in range(HEADS):
        for part, ref in enumerate((k_ref, v_ref)):
            twin_copy(ref, part, head).wait_send()
    twin_queries().wait_send()

    @pl.loop(0, HEADS)
    def _(head):
        for role in range(ROLES):
            for block in needed(role):
                pass_on(role, block, head, finish)
        own_result(head).wait()
        twin_result(head).wait()


def on_device(queries, keys, values, span_order):
    rows = queries.shape[0]
    return pl.pallas_call(
        kernel,
        out_shape=jax.ShapeDtypeStruct(queries.shape, jnp.bfloat16),
        in_specs=[pl.BlockSpec(memory_space=pltpu.SMEM)] + [pl.BlockSpec(memory_space=pl.ANY)] * 3,
        out_specs=pl.BlockSpec(memory_space=pl.ANY),
        scratch_shapes=[
            pltpu.VMEM((ROLES, BLOCKS, HEADS, 2, rows, HEAD), jnp.bfloat16),
            pltpu.VMEM((2, rows, HEADS * QUARTER), jnp.bfloat16),
            pltpu.VMEM((2, HEADS, rows, QUARTER), jnp.bfloat16),
            pltpu.VMEM((2, HEADS, QUARTER, HEAD), jnp.float32),
            pltpu.VMEM((2, HEADS, QUARTER, HEAD), jnp.float32),
            pltpu.VMEM((2, HEADS, QUARTER, HEAD), jnp.float32),
            pltpu.VMEM((ROLES, 2, 2, rows, HEAD), jnp.float32),
            pltpu.SemaphoreType.DMA((ROLES, BLOCKS, HEADS, ROLES - 1)),
            pltpu.SemaphoreType.DMA((ROLES, BLOCKS, HEADS)),
            pltpu.SemaphoreType.DMA((HEADS, 2)),
            pltpu.SemaphoreType.DMA((2,)),
            pltpu.SemaphoreType.DMA,
            pltpu.SemaphoreType.DMA((3, HEADS)),
        ],
        compiler_params=pltpu.CompilerParams(
            collective_id=0, has_side_effects=True, vmem_limit_bytes=48 * 2**20
        ),
        name="attend_window",
    )(span_order, queries, keys, values)


def solution(mesh):
    rows = P(("outer", "inner"), None)
    return jax.shard_map(
        on_device,
        mesh=mesh,
        in_specs=(rows, rows, rows, P()),
        out_specs=rows,
        check_vma=False,
    )
```

```python
import functools
import math

import jax
import jax.numpy as jnp
from jax import lax
from jax.experimental import pallas as pl
from jax.experimental.pallas import tpu as pltpu
from jax.sharding import PartitionSpec as P

ROLES = 6
BLOCKS = 2
HEADS = 4
GROUP = 4
HEAD = 128
QUARTER = GROUP * HEAD
MESH = pl.DeviceIdType.MESH
MASKED = -1e30

OFFSETS = ((-1, 0), (-1, 1), (-1, 2), (0, -2), (0, -1), (0, 1), (0, 2), (1, -1), (1, 0), (1, 1), (1, 2),)

WIDE = 2
PIECES = HEADS // WIDE

STEPS = (
    (0x403, 0x114, 0x413, 0x301, 0x349, 0xC, 0x1595C, 0x311, 0x15A59, 0x44, 0x4B, 0x4A, 0x25D, 0x5B, 0xDA, 0xCD,),
    (0x11A09, 0x2C5A, 0x104, 0x15A19, 0x441, 0x3, 0x44B, 0x4C, 0x51, 0x1B, 0x4A, 0x1C, 0x53, 0x54, 0xDD, 0xCD,),
    (0x301, 0x411, 0x16259, 0x11A4D, 0x1B, 0x2249, 0x30C, 0x144, 0xB, 0x14, 0x2B5C, 0x43, 0x5D, 0x53, 0xCA, 0xDA,),
    (0x2C1B, 0x209, 0x403, 0x453, 0x441, 0x311, 0x15A1C, 0x354, 0x5D, 0x59, 0x4A, 0x104, 0x4B, 0xDA, 0x4D, 0xCC,),
    (0x401, 0x419, 0x49, 0x40B, 0x51, 0x113, 0x30C, 0x5B, 0x5A, 0x344, 0x314, 0x4A, 0x5C, 0x43, 0xDD, 0xCD,),
    (0x2319, 0x50B, 0x401, 0x41B, 0x451, 0x49, 0x15A, 0x1C, 0x54A, 0x104, 0x2B4C, 0x54, 0x43, 0x5D, 0xCD, 0xD3,),
    (0x401, 0x1614A, 0x314, 0x2103, 0x44D, 0x5A, 0x349, 0x519, 0x51, 0x4B, 0x304, 0x13, 0x5C, 0x5B, 0xCC, 0xDD,),
    (0x2C09, 0x4A, 0x441, 0x5D, 0x2311, 0xB, 0x43, 0x13, 0x5B, 0x1904, 0x59, 0x1C, 0x24C, 0x54, 0xDA, 0xCD,),
    (0x104, 0x50B, 0x114, 0x13, 0x443, 0x15C, 0x311, 0x54C, 0x24D, 0x5B, 0x54A, 0x259, 0x1, 0xC9, 0x5D, 0xDA,),
    (0x40B, 0x11C, 0x2319, 0x50C, 0x154, 0x5D, 0x1, 0x451, 0x1B, 0x4D, 0x44, 0x55A, 0xD3, 0x43, 0x49, 0xCA,),
    (0x413, 0x2209, 0x25B, 0x2219, 0x14, 0x51, 0x35C, 0x3, 0x14A, 0x4, 0x4B, 0x4C, 0x24D, 0xC1, 0x5D, 0xDA,),
    (0x1A09, 0x411, 0x295A, 0x1B, 0x59, 0x31C, 0xC, 0xB, 0x54, 0x344, 0x294A, 0x4D, 0x43, 0x53, 0xDD, 0xC1,),
    (0x401, 0x413, 0x411, 0x45B, 0x2259, 0x49, 0x304, 0x3, 0x34C, 0x14, 0x55C, 0x54A, 0x5A, 0xDD, 0x4D, 0xCB,),
    (0x409, 0x225D, 0x30C, 0x2A1C, 0x19, 0x51, 0x344, 0x54A, 0xB, 0x354, 0x1B, 0x53, 0x4D, 0x43, 0xC1, 0xDA,),
    (0x401, 0x4A, 0x249, 0x519, 0x304, 0x3, 0x4C, 0x4D, 0xCB, 0x14, 0x25C, 0x55A, 0x13, 0x5B, 0x5D, 0xD1,),
    (0x409, 0x44D, 0x103, 0x219, 0x4A, 0x13, 0x5A, 0x4B, 0x2351, 0x1A0C, 0x191C, 0x5B, 0x344, 0x5D, 0xD4, 0xC1,),
)

FIRST = (
    (0x288,),
    (0x1926B,),
    (0x688,),
    (0x2E9,),
    (0x688,),
    (0x253,),
    (0x8A0,),
    (0x263,),
    (0x698,),
    (0x8C9,),
    (0x288,),
    (0x6C9,),
    (0x222,),
    (0x6D92C9,),
    (0x622,),
    (0x453,),
)
FIRST_COUNT = (2, 3, 2, 2, 2, 2, 2, 2, 2, 2, 2, 2, 2, 4, 2, 2)
THEN = (
    (0x68964B, 0x0,),
    (0x22288, 0x0,),
    (0x29B2D1, 0x0,),
    (0x251288, 0x0,),
    (0x212C9A5B, 0xA,),
    (0x288, 0x0,),
    (0x9863, 0x0,),
    (0x1A898, 0x0,),
    (0xA2C9, 0x0,),
    (0x2D880A, 0x0,),
    (0x96D12E9, 0x0,),
    (0xB4D1698, 0xA,),
    (0x1B8D92C9, 0x0,),
    (0x2A0, 0x0,),
    (0x8E9, 0x0,),
    (0x186612A0, 0x1A,),
)
THEN_COUNT = (4, 3, 4, 4, 6, 2, 3, 3, 3, 4, 5, 6, 5, 2, 2, 6)

SENDS = (19, 17, 20, 18, 15, 15, 16, 13, 15, 14, 16, 17, 17, 15, 10, 19)
FAN = 3

SEEN = {
    0: ((0,), (0, 1)),
    1: ((0, 1), (0, 1)),
    2: ((1,), ()),
    3: ((0,), (0, 1)),
    4: ((0, 1), (0, 1)),
    5: ((1,), ()),
}


def pick(choices, at):
    value = jnp.int32(choices[0])
    for index in range(1, len(choices)):
        value = jnp.where(at == index, choices[index], value)
    return value


def bits(value, low, count):
    return lax.shift_right_logical(value, jnp.int32(low)) & ((1 << count) - 1)


def place(role, piece, block):
    return (role * PIECES + piece) * BLOCKS + block


def kernel(spans_ref, q_ref, k_ref, v_ref, o_ref, order_ref, held, qbuf, obuf, peak, total, acc, hidden,
           send_sem, recv_sem, swap_sem, q_sem, qswap_sem, o_sem, order_sem):
    n_outer = lax.axis_size("outer")
    n_chips = lax.axis_size("inner") // 2
    outer = lax.axis_index("outer")
    inner = lax.axis_index("inner")
    chip, core = inner // 2, inner % 2
    kind = ((outer % 2) * 4 + chip % 4) * 2 + core
    other = 1 - core

    def device(d_outer, d_chip):
        return (
            (outer + d_outer + n_outer) & (n_outer - 1),
            ((chip + d_chip + n_chips) & (n_chips - 1)) * 2 + core,
        )

    twin = (outer, chip * 2 + other)

    barrier = pltpu.get_barrier_semaphore()
    for d_outer, d_chip in OFFSETS:
        pl.semaphore_signal(barrier, 1, device_id=device(-d_outer, -d_chip), device_id_type=MESH)
    pl.semaphore_signal(barrier, 1, device_id=twin, device_id_type=MESH)

    def own_copy(ref, part, head):
        columns = pl.ds((core * HEADS + head) * HEAD, HEAD)
        return pltpu.make_async_copy(
            ref.at[:, columns], held.at[place(0, head // WIDE, core), head % WIDE, part], recv_sem.at[place(0, head // WIDE, core)]
        )

    def twin_copy(ref, part, head):
        columns = pl.ds((other * HEADS + head) * HEAD, HEAD)
        return pltpu.make_async_remote_copy(
            src_ref=ref.at[:, columns],
            dst_ref=held.at[place(0, head // WIDE, core), head % WIDE, part],
            send_sem=swap_sem.at[head, part],
            recv_sem=recv_sem.at[place(0, head // WIDE, core)],
            device_id=twin,
            device_id_type=MESH,
        )

    width = HEADS * QUARTER

    def own_queries():
        return pltpu.make_async_copy(
            q_ref.at[:, pl.ds(core * width, width)], qbuf.at[core], q_sem.at[core]
        )

    def twin_queries():
        return pltpu.make_async_remote_copy(
            src_ref=q_ref.at[:, pl.ds(other * width, width)],
            dst_ref=qbuf.at[core],
            send_sem=qswap_sem,
            recv_sem=q_sem.at[core],
            device_id=twin,
            device_id_type=MESH,
        )

    for head in range(HEADS):
        for part, ref in enumerate((k_ref, v_ref)):
            own_copy(ref, part, head).start()
    own_queries().start()
    spans = pltpu.make_async_copy(spans_ref, order_ref, order_sem)
    spans.start()

    def hidden_tile(role, query_core, key_core):
        d_outer, d_chip = role // 3, role % 3
        at_outer, at_inner = device(-d_outer, -d_chip)
        source = at_outer * (2 * n_chips) + (at_inner - core) + key_core
        mine = outer * (2 * n_chips) + chip * 2 + query_core
        row = lax.broadcasted_iota(jnp.int32, (HEAD, HEAD), 0)
        column = lax.broadcasted_iota(jnp.int32, (HEAD, HEAD), 1)
        half = HEAD // 2
        row_at = jnp.where(row < half, order_ref[2 * mine] * half, order_ref[2 * mine + 1] * half - half) + row
        column_at = (
            jnp.where(column < half, order_ref[2 * source] * half, order_ref[2 * source + 1] * half - half) + column
        )
        return jnp.where(column_at <= row_at, 0.0, MASKED)

    def copy_on(role, block, piece, there):
        far, far_there = (role + 5) >> 3, (there + 5) >> 3
        to = device(far_there - far, (there - 3 * far_there) - (role - 3 * far))
        return pltpu.make_async_remote_copy(
            src_ref=held.at[place(role, piece, block)],
            dst_ref=held.at[place(there, piece, block)],
            send_sem=send_sem,
            recv_sem=recv_sem.at[place(there, piece, block)],
            device_id=to,
            device_id_type=MESH,
        )

    def arrive(slot):
        chunk = held.at[slot]
        pltpu.make_async_copy(chunk, chunk, recv_sem.at[slot]).wait()

    def own_sends(words, count):
        @pl.loop(0, count)
        def _(step):
            code = lax.shift_right_logical(pick(words, lax.div(step, 5)), lax.rem(step, 5) * 6)
            copy_on(0, bits(code, 0, 1), bits(code, 1, 2), bits(code, 3, 3)).start()

    def column(table):
        return [pick([row[at] for row in table], kind) for at in range(len(table[0]))]

    def pass_on(code, role, block, piece, at=0):
        if at == FAN:
            return
        there = bits(code, 8 + 3 * at, 3)

        @pl.when(there > 0)
        def _():
            copy_on(role, block, piece, there).start()
            pass_on(code, role, block, piece, at + 1)

    steps = column(STEPS)
    first, then = column(FIRST), column(THEN)
    first_count, then_count = pick(FIRST_COUNT, kind), pick(THEN_COUNT, kind)
    sends = pick(SENDS, kind)

    pl.semaphore_wait(barrier, len(OFFSETS) + 1)

    for head in range(HEADS):
        for part, ref in enumerate((k_ref, v_ref)):
            twin_copy(ref, part, head).start()

    for piece in range(PIECES):
        arrive(place(0, piece, core))
    own_sends(first, first_count)
    for piece in range(PIECES):
        arrive(place(0, piece, other))
    own_sends(then, then_count)
    twin_queries().start()

    spans.wait()
    for role in range(ROLES):
        for query_core in range(2):
            for key_core in SEEN[role][query_core]:
                hidden[role, query_core, key_core] = hidden_tile(role, query_core, key_core)

    scale = math.log2(math.e) / math.sqrt(HEAD)

    def attend(seen_by, role, piece, wide, fresh=False):
        head = piece * WIDE + wide

        def gather(part, seen):
            return jnp.concatenate([held[place(role, piece, block), wide, part] for block in seen], axis=0)

        for query_core in range(2):
            seen = seen_by[query_core]
            if not seen:
                continue
            queries = jnp.concatenate(
                [
                    qbuf[query_core, :, pl.ds(pl.multiple_of((head * GROUP + at) * HEAD, HEAD), HEAD)]
                    for at in range(GROUP)
                ],
                axis=0,
            )
            score = lax.dot_general(
                queries,
                gather(0, seen),
                (((1,), (1,)), ((), ())),
                preferred_element_type=jnp.float32,
            )
            scores = [
                (
                    score[:, n * HEAD : (n + 1) * HEAD].reshape(GROUP, HEAD, HEAD) * scale
                    + hidden[role, query_core, block][None]
                ).reshape(QUARTER, HEAD)
                for n, block in enumerate(seen)
            ]
            top = scores[0] if len(seen) == 1 else jnp.maximum(scores[0], scores[1])
            top = jnp.broadcast_to(jnp.max(top, axis=1, keepdims=True), (QUARTER, HEAD))
            if not fresh:
                old = peak[query_core, head]
                top = jnp.maximum(old, top)
                factor = jnp.exp2(old - top)
            weights = [jnp.exp2(part - top) for part in scores]
            summed = weights[0] if len(seen) == 1 else weights[0] + weights[1]
            update = jnp.dot(
                jnp.concatenate([weight.astype(jnp.bfloat16) for weight in weights], axis=1),
                gather(1, seen),
                preferred_element_type=jnp.float32,
            )
            if not fresh:
                summed = total[query_core, head] * factor + summed
                update = acc[query_core, head] * factor + update
            peak[query_core, head] = top
            total[query_core, head] = summed
            acc[query_core, head] = update

    for query_core in range(2):
        pltpu.make_async_copy(qbuf.at[query_core], qbuf.at[query_core], q_sem.at[query_core]).wait()

    @pl.loop(0, HEADS)
    def _(head):
        attend(SEEN[0], 0, head // WIDE, head % WIDE, fresh=True)

    def own_result(head):
        columns = pl.ds((core * HEADS + head) * QUARTER, QUARTER)
        return pltpu.make_async_copy(obuf.at[core, head], o_ref.at[:, columns], o_sem.at[0, head])

    def twin_result(head):
        columns = pl.ds((core * HEADS + head) * QUARTER, QUARTER)
        return pltpu.make_async_remote_copy(
            src_ref=obuf.at[other, head],
            dst_ref=o_ref.at[:, columns],
            send_sem=o_sem.at[1, head],
            recv_sem=o_sem.at[2, head],
            device_id=twin,
            device_id_type=MESH,
        )

    def conclude(head):
        for query_core in range(2):
            for at in range(GROUP):
                rows = pl.ds(at * HEAD, HEAD)
                sums = jnp.sum(total[query_core, head, rows], axis=1, keepdims=True)
                result = acc[query_core, head, rows] / sums
                obuf[query_core, head, :, at * HEAD : (at + 1) * HEAD] = result.astype(jnp.bfloat16)
        twin_result(head).start()
        own_result(head).start()

    @pl.loop(0, len(steps))
    def _(step):
        code = pick(steps, step)
        role, block, piece = bits(code, 0, 3), bits(code, 3, 1), bits(code, 4, 2)
        arrive(place(role, piece, block))
        pass_on(code, role, block, piece)
        complete = bits(code, 6, 1)
        for like in (1, 2, 3):
            same = (role == like) | (role == like + 3) if like < 3 else role == 3

            @pl.when((complete == 1) & same)
            def _():
                @pl.loop(0, WIDE)
                def _(wide):
                    attend(SEEN[like], role, piece, wide)

        @pl.when(bits(code, 7, 1) == 1)
        def _():
            @pl.loop(0, WIDE)
            def _(wide):
                conclude(piece * WIDE + wide)

    for head in range(HEADS):
        for part, ref in enumerate((k_ref, v_ref)):
            twin_copy(ref, part, head).wait_send()
    twin_queries().wait_send()
    for count in sorted(set(SENDS)):
        @pl.when(sends == count)
        def _():
            sent = held.at[pl.ds(0, count)]
            pltpu.make_async_copy(sent, sent, send_sem).wait()

    @pl.loop(0, HEADS)
    def _(head):
        own_result(head).wait()
        twin_result(head).wait()


def on_device(queries, keys, values, span_order):
    rows = queries.shape[0]
    return pl.pallas_call(
        kernel,
        out_shape=jax.ShapeDtypeStruct(queries.shape, jnp.bfloat16),
        in_specs=[pl.BlockSpec(memory_space=pltpu.HBM)] * 4,
        out_specs=pl.BlockSpec(memory_space=pl.ANY),
        scratch_shapes=[
            pltpu.SMEM(span_order.shape, jnp.int32),
            pltpu.VMEM((ROLES * PIECES * BLOCKS, WIDE, 2, rows, HEAD), jnp.bfloat16),
            pltpu.VMEM((2, rows, HEADS * QUARTER), jnp.bfloat16),
            pltpu.VMEM((2, HEADS, rows, QUARTER), jnp.bfloat16),
            pltpu.VMEM((2, HEADS, QUARTER, HEAD), jnp.float32),
            pltpu.VMEM((2, HEADS, QUARTER, HEAD), jnp.float32),
            pltpu.VMEM((2, HEADS, QUARTER, HEAD), jnp.float32),
            pltpu.VMEM((ROLES, 2, 2, rows, HEAD), jnp.float32),
            pltpu.SemaphoreType.DMA,
            pltpu.SemaphoreType.DMA((ROLES * PIECES * BLOCKS,)),
            pltpu.SemaphoreType.DMA((HEADS, 2)),
            pltpu.SemaphoreType.DMA((2,)),
            pltpu.SemaphoreType.DMA,
            pltpu.SemaphoreType.DMA((3, HEADS)),
            pltpu.SemaphoreType.DMA,
        ],
        compiler_params=pltpu.CompilerParams(
            collective_id=0, has_side_effects=True, vmem_limit_bytes=52 * 2**20
        ),
        name="attend_window",
    )(*(pltpu.with_memory_space_constraint(one, pltpu.HBM) for one in (span_order, queries, keys, values)))


def solution(mesh):
    rows = P(("outer", "inner"), None)
    return jax.shard_map(
        on_device,
        mesh=mesh,
        in_specs=(rows, rows, rows, P()),
        out_specs=rows,
        check_vma=False,
    )
```

```python
import functools
import math

import jax
import jax.numpy as jnp
from jax import lax
from jax.experimental import pallas as pl
from jax.experimental.pallas import tpu as pltpu
from jax.sharding import PartitionSpec as P

ROLES = 6
BLOCKS = 2
HEADS = 4
GROUP = 4
HEAD = 128
QUARTER = GROUP * HEAD
MESH = pl.DeviceIdType.MESH
MASKED = -1e30

OFFSETS = ((-1, -1), (-1, 0), (-1, 1), (-1, 2), (0, -2), (0, -1), (0, 1), (0, 2), (1, -2), (1, -1), (1, 0), (1, 1), (1, 2),)

WIDE = 2
PIECES = HEADS // WIDE

STEPS = (
    (0x304, 0xB, 0x2301, 0x1914, 0x411, 0x43, 0x115D, 0x54C, 0x13, 0x249, 0x59, 0x55C, 0x54A, 0x5B, 0xCD, 0xDA,),
    (0x51B, 0x1A19, 0x53, 0xC, 0x4A, 0x9, 0x441, 0xB, 0x5A, 0x43, 0x5D, 0x44, 0x51, 0xCD, 0x14, 0xDC,),
    (0x411, 0x51B, 0x1904, 0x509, 0x53, 0x314, 0x59, 0x1615A, 0x2A4C, 0x3, 0x4D, 0x15A5C, 0x4A, 0x41, 0xCB, 0xDD,),
    (0x2209, 0x2C0B, 0x2219, 0x214D, 0x413, 0x34A, 0x451, 0x30C, 0x41, 0x5B, 0x5A, 0x44, 0x225D, 0x4C3, 0x14, 0xDC,),
    (0x401, 0x403, 0x2C19, 0x49, 0x51, 0x41B, 0x1C, 0x304, 0x54, 0x53, 0x2B4C, 0x4B, 0x4D, 0x5D, 0xCA, 0xDA,),
    (0x2B09, 0x411, 0x59, 0x403, 0x441, 0x4A, 0x2B1C, 0xC, 0x4B, 0x55A, 0x154, 0x5D, 0x1B, 0x4D, 0xD3, 0xC4,),
    (0x401, 0x14A, 0x5A, 0x19, 0x211B, 0x45D, 0x4, 0x314, 0x103, 0xAD14C, 0x53, 0x5C, 0xD1, 0x49, 0x4D, 0xCB,),
    (0x1615A, 0x2A19, 0x351, 0x9, 0x4D, 0x15A0C, 0xB, 0x1B, 0x1A1C, 0x144, 0x43, 0x354, 0x5D, 0xD3, 0x41, 0xCA,),
    (0x403, 0x41B, 0x4B, 0x1590C, 0x44, 0x53, 0x11, 0x309, 0x259, 0x14, 0x25D, 0x5C, 0xDA, 0x41, 0x4A, 0xCD,),
    (0x291C, 0x224D, 0x2B19, 0x1B, 0x10C, 0x3, 0x4B, 0x2301, 0x2351, 0x5D, 0x249, 0x154, 0x4A, 0xC4, 0x53, 0xDA,),
    (0x411, 0x413, 0x409, 0x314, 0x14A, 0x459, 0x41, 0x50B, 0x104, 0x43, 0x2A5C, 0x5D, 0x4D, 0x5B, 0xCC, 0xDA,),
    (0x224D, 0x409, 0x3, 0x2B0C, 0x2341, 0x1C, 0x44B, 0x411, 0x459, 0x44, 0x354, 0x1B, 0x5D, 0x53, 0xCA, 0xDA,),
    (0x401, 0x413, 0x411, 0x449, 0x59, 0xB, 0x30C, 0x344, 0x43, 0x14, 0x5B, 0x35C, 0x224D, 0x5D, 0xCA, 0xDA,),
    (0x419, 0x41B, 0x9, 0x341, 0x403, 0x15A, 0x1C, 0x54A, 0x4D, 0x354, 0xC, 0x453, 0x4B, 0xC4, 0x5D, 0xD1,),
    (0x113, 0x411, 0x15A, 0x25B, 0x4A, 0x1, 0x304, 0x3, 0x2B1C, 0x154, 0x114C, 0x59, 0x4D, 0xDD, 0x4B, 0xC9,),
    (0x14A, 0x2C19, 0x5A, 0x413, 0x451, 0x103, 0x9, 0x5B, 0x35D, 0x1C, 0x4B, 0x30C, 0x144, 0x24D, 0xD4, 0xC1,),
)

FIRST = (
    (0x298,),
    (0x2C9,),
    (0x688,),
    (0x253,),
    (0x688,),
    (0x1B2E9,),
    (0x21A,),
    (0x8E9,),
    (0x80A,),
    (0x6D1253,),
    (0x288,),
    (0x1164B,),
    (0x60A,),
    (0x84B,),
    (0x8A0,),
    (0x2E9,),
)
FIRST_COUNT = (2, 2, 2, 2, 2, 3, 2, 2, 2, 4, 2, 3, 2, 2, 2, 2)
THEN = (
    (0x2D96C9,),
    (0x1821B80A,),
    (0xA4D12E1,),
    (0x1820A,),
    (0x2D9863,),
    (0x960A,),
    (0x85B,),
    (0x61A,),
    (0x192C9,),
    (0x1A288,),
    (0x1169325B,),
    (0x1321A,),
    (0x21B86B,),
    (0x9298,),
    (0x216D1,),
    (0x19288,),
)
THEN_COUNT = (4, 5, 5, 3, 4, 3, 2, 2, 3, 3, 5, 3, 4, 3, 3, 3)

SENDS = (18, 11, 21, 20, 14, 15, 15, 17, 13, 20, 17, 17, 15, 13, 15, 15)
FAN = 4

SEEN = {
    0: ((0,), (0, 1)),
    1: ((0, 1), (0, 1)),
    2: ((1,), ()),
    3: ((0,), (0, 1)),
    4: ((0, 1), (0, 1)),
    5: ((1,), ()),
}


def pick(choices, at):
    value = jnp.int32(choices[0])
    for index in range(1, len(choices)):
        value = jnp.where(at == index, choices[index], value)
    return value


def bits(value, low, count):
    return lax.shift_right_logical(value, jnp.int32(low)) & ((1 << count) - 1)


def place(role, piece, block):
    return (role * PIECES + piece) * BLOCKS + block


def kernel(spans_ref, q_ref, k_ref, v_ref, o_ref, order_ref, held, qbuf, obuf, peak, total, acc, hidden,
           send_sem, recv_sem, swap_sem, q_sem, qswap_sem, o_sem, order_sem):
    n_outer = lax.axis_size("outer")
    n_chips = lax.axis_size("inner") // 2
    outer = lax.axis_index("outer")
    inner = lax.axis_index("inner")
    chip, core = inner // 2, inner % 2
    kind = ((outer % 2) * 4 + chip % 4) * 2 + core
    other = 1 - core

    def device(d_outer, d_chip):
        return (
            (outer + d_outer + n_outer) & (n_outer - 1),
            ((chip + d_chip + n_chips) & (n_chips - 1)) * 2 + core,
        )

    twin = (outer, chip * 2 + other)

    barrier = pltpu.get_barrier_semaphore()
    for d_outer, d_chip in OFFSETS:
        pl.semaphore_signal(barrier, 1, device_id=device(-d_outer, -d_chip), device_id_type=MESH)
    pl.semaphore_signal(barrier, 1, device_id=twin, device_id_type=MESH)

    def own_copy(ref, part, head):
        columns = pl.ds((core * HEADS + head) * HEAD, HEAD)
        return pltpu.make_async_copy(
            ref.at[:, columns], held.at[place(0, head // WIDE, core), head % WIDE, part], recv_sem.at[place(0, head // WIDE, core)]
        )

    def twin_copy(ref, part, head):
        columns = pl.ds((other * HEADS + head) * HEAD, HEAD)
        return pltpu.make_async_remote_copy(
            src_ref=ref.at[:, columns],
            dst_ref=held.at[place(0, head // WIDE, core), head % WIDE, part],
            send_sem=swap_sem.at[head, part],
            recv_sem=recv_sem.at[place(0, head // WIDE, core)],
            device_id=twin,
            device_id_type=MESH,
        )

    width = HEADS * QUARTER

    def own_queries():
        return pltpu.make_async_copy(
            q_ref.at[:, pl.ds(core * width, width)], qbuf.at[core], q_sem.at[core]
        )

    def twin_queries():
        return pltpu.make_async_remote_copy(
            src_ref=q_ref.at[:, pl.ds(other * width, width)],
            dst_ref=qbuf.at[core],
            send_sem=qswap_sem,
            recv_sem=q_sem.at[core],
            device_id=twin,
            device_id_type=MESH,
        )

    for head in range(HEADS):
        for part, ref in enumerate((k_ref, v_ref)):
            own_copy(ref, part, head).start()
    own_queries().start()
    spans = pltpu.make_async_copy(spans_ref, order_ref, order_sem)
    spans.start()

    def hidden_tile(role, query_core, key_core):
        d_outer, d_chip = role // 3, role % 3
        at_outer, at_inner = device(-d_outer, -d_chip)
        source = at_outer * (2 * n_chips) + (at_inner - core) + key_core
        mine = outer * (2 * n_chips) + chip * 2 + query_core
        row = lax.broadcasted_iota(jnp.int32, (HEAD, HEAD), 0)
        column = lax.broadcasted_iota(jnp.int32, (HEAD, HEAD), 1)
        half = HEAD // 2
        row_at = jnp.where(row < half, order_ref[2 * mine] * half, order_ref[2 * mine + 1] * half - half) + row
        column_at = (
            jnp.where(column < half, order_ref[2 * source] * half, order_ref[2 * source + 1] * half - half) + column
        )
        return jnp.where(column_at <= row_at, 0.0, MASKED)

    def copy_on(role, block, piece, there):
        far, far_there = (role + 5) >> 3, (there + 5) >> 3
        to = device(far_there - far, (there - 3 * far_there) - (role - 3 * far))
        return pltpu.make_async_remote_copy(
            src_ref=held.at[place(role, piece, block)],
            dst_ref=held.at[place(there, piece, block)],
            send_sem=send_sem,
            recv_sem=recv_sem.at[place(there, piece, block)],
            device_id=to,
            device_id_type=MESH,
        )

    def arrive(slot):
        chunk = held.at[slot]
        pltpu.make_async_copy(chunk, chunk, recv_sem.at[slot]).wait()

    def own_sends(words, count):
        @pl.loop(0, count)
        def _(step):
            code = lax.shift_right_logical(pick(words, lax.div(step, 5)), lax.rem(step, 5) * 6)
            copy_on(0, bits(code, 0, 1), bits(code, 1, 2), bits(code, 3, 3)).start()

    def column(table):
        return [pick([row[at] for row in table], kind) for at in range(len(table[0]))]

    def pass_on(code, role, block, piece, at=0):
        if at == FAN:
            return
        there = bits(code, 8 + 3 * at, 3)

        @pl.when(there > 0)
        def _():
            copy_on(role, block, piece, there).start()
            pass_on(code, role, block, piece, at + 1)

    steps = column(STEPS)
    first, then = column(FIRST), column(THEN)
    first_count, then_count = pick(FIRST_COUNT, kind), pick(THEN_COUNT, kind)
    sends = pick(SENDS, kind)

    pl.semaphore_wait(barrier, len(OFFSETS) + 1)

    for head in range(HEADS):
        for part, ref in enumerate((k_ref, v_ref)):
            twin_copy(ref, part, head).start()

    for piece in range(PIECES):
        arrive(place(0, piece, core))
    own_sends(first, first_count)
    for piece in range(PIECES):
        arrive(place(0, piece, other))
    own_sends(then, then_count)
    twin_queries().start()

    spans.wait()
    for role in range(ROLES):
        for query_core in range(2):
            for key_core in SEEN[role][query_core]:
                hidden[role, query_core, key_core] = hidden_tile(role, query_core, key_core)

    scale = math.log2(math.e) / math.sqrt(HEAD)

    def attend(seen_by, role, piece, wide, fresh=False):
        head = piece * WIDE + wide

        def gather(part, seen):
            return jnp.concatenate([held[place(role, piece, block), wide, part] for block in seen], axis=0)

        for query_core in range(2):
            seen = seen_by[query_core]
            if not seen:
                continue
            queries = jnp.concatenate(
                [
                    qbuf[query_core, :, pl.ds(pl.multiple_of((head * GROUP + at) * HEAD, HEAD), HEAD)]
                    for at in range(GROUP)
                ],
                axis=0,
            )
            score = lax.dot_general(
                queries,
                gather(0, seen),
                (((1,), (1,)), ((), ())),
                preferred_element_type=jnp.float32,
            )
            scores = [
                (
                    score[:, n * HEAD : (n + 1) * HEAD].reshape(GROUP, HEAD, HEAD) * scale
                    + hidden[role, query_core, block][None]
                ).reshape(QUARTER, HEAD)
                for n, block in enumerate(seen)
            ]
            top = scores[0] if len(seen) == 1 else jnp.maximum(scores[0], scores[1])
            top = jnp.broadcast_to(jnp.max(top, axis=1, keepdims=True), (QUARTER, HEAD))
            if not fresh:
                old = peak[query_core, head]
                top = jnp.maximum(old, top)
                factor = jnp.exp2(old - top)
            weights = [jnp.exp2(part - top) for part in scores]
            summed = weights[0] if len(seen) == 1 else weights[0] + weights[1]
            update = jnp.dot(
                jnp.concatenate([weight.astype(jnp.bfloat16) for weight in weights], axis=1),
                gather(1, seen),
                preferred_element_type=jnp.float32,
            )
            if not fresh:
                summed = total[query_core, head] * factor + summed
                update = acc[query_core, head] * factor + update
            peak[query_core, head] = top
            total[query_core, head] = summed
            acc[query_core, head] = update

    for query_core in range(2):
        pltpu.make_async_copy(qbuf.at[query_core], qbuf.at[query_core], q_sem.at[query_core]).wait()

    @pl.loop(0, HEADS)
    def _(head):
        attend(SEEN[0], 0, head // WIDE, head % WIDE, fresh=True)

    def own_result(head):
        columns = pl.ds((core * HEADS + head) * QUARTER, QUARTER)
        return pltpu.make_async_copy(obuf.at[core, head], o_ref.at[:, columns], o_sem.at[0, head])

    def twin_result(head):
        columns = pl.ds((core * HEADS + head) * QUARTER, QUARTER)
        return pltpu.make_async_remote_copy(
            src_ref=obuf.at[other, head],
            dst_ref=o_ref.at[:, columns],
            send_sem=o_sem.at[1, head],
            recv_sem=o_sem.at[2, head],
            device_id=twin,
            device_id_type=MESH,
        )

    def conclude(head):
        for query_core in range(2):
            for at in range(GROUP):
                rows = pl.ds(at * HEAD, HEAD)
                sums = jnp.sum(total[query_core, head, rows], axis=1, keepdims=True)
                result = acc[query_core, head, rows] / sums
                obuf[query_core, head, :, at * HEAD : (at + 1) * HEAD] = result.astype(jnp.bfloat16)
        twin_result(head).start()
        own_result(head).start()

    @pl.loop(0, len(steps))
    def _(step):
        code = pick(steps, step)
        role, block, piece = bits(code, 0, 3), bits(code, 3, 1), bits(code, 4, 2)
        arrive(place(role, piece, block))
        pass_on(code, role, block, piece)
        complete = bits(code, 6, 1)
        for like in (1, 2, 3):
            same = (role == like) | (role == like + 3) if like < 3 else role == 3

            @pl.when((complete == 1) & same)
            def _():
                @pl.loop(0, WIDE)
                def _(wide):
                    attend(SEEN[like], role, piece, wide)

        @pl.when(bits(code, 7, 1) == 1)
        def _():
            @pl.loop(0, WIDE)
            def _(wide):
                conclude(piece * WIDE + wide)

    for head in range(HEADS):
        for part, ref in enumerate((k_ref, v_ref)):
            twin_copy(ref, part, head).wait_send()
    twin_queries().wait_send()
    for count in sorted(set(SENDS)):
        @pl.when(sends == count)
        def _():
            sent = held.at[pl.ds(0, count)]
            pltpu.make_async_copy(sent, sent, send_sem).wait()

    @pl.loop(0, HEADS)
    def _(head):
        own_result(head).wait()
        twin_result(head).wait()


def on_device(queries, keys, values, span_order):
    rows = queries.shape[0]
    return pl.pallas_call(
        kernel,
        out_shape=jax.ShapeDtypeStruct(queries.shape, jnp.bfloat16),
        in_specs=[pl.BlockSpec(memory_space=pltpu.HBM)] * 4,
        out_specs=pl.BlockSpec(memory_space=pl.ANY),
        scratch_shapes=[
            pltpu.SMEM(span_order.shape, jnp.int32),
            pltpu.VMEM((ROLES * PIECES * BLOCKS, WIDE, 2, rows, HEAD), jnp.bfloat16),
            pltpu.VMEM((2, rows, HEADS * QUARTER), jnp.bfloat16),
            pltpu.VMEM((2, HEADS, rows, QUARTER), jnp.bfloat16),
            pltpu.VMEM((2, HEADS, QUARTER, HEAD), jnp.float32),
            pltpu.VMEM((2, HEADS, QUARTER, HEAD), jnp.float32),
            pltpu.VMEM((2, HEADS, QUARTER, HEAD), jnp.float32),
            pltpu.VMEM((ROLES, 2, 2, rows, HEAD), jnp.float32),
            pltpu.SemaphoreType.DMA,
            pltpu.SemaphoreType.DMA((ROLES * PIECES * BLOCKS,)),
            pltpu.SemaphoreType.DMA((HEADS, 2)),
            pltpu.SemaphoreType.DMA((2,)),
            pltpu.SemaphoreType.DMA,
            pltpu.SemaphoreType.DMA((3, HEADS)),
            pltpu.SemaphoreType.DMA,
        ],
        compiler_params=pltpu.CompilerParams(
            collective_id=0, has_side_effects=True, vmem_limit_bytes=52 * 2**20
        ),
        name="attend_window",
    )(*(pltpu.with_memory_space_constraint(one, pltpu.HBM) for one in (span_order, queries, keys, values)))


def solution(mesh):
    rows = P(("outer", "inner"), None)
    return jax.shard_map(
        on_device,
        mesh=mesh,
        in_specs=(rows, rows, rows, P()),
        out_specs=rows,
        check_vma=False,
    )
```

```python
import functools
import math

import jax
import jax.numpy as jnp
from jax import lax
from jax.experimental import pallas as pl
from jax.experimental.pallas import tpu as pltpu
from jax.sharding import PartitionSpec as P

ROLES = 6
BLOCKS = 2
HEADS = 4
GROUP = 4
HEAD = 128
QUARTER = GROUP * HEAD
MESH = pl.DeviceIdType.MESH
MASKED = -1e30

OFFSETS = ((-1, -1), (-1, 0), (-1, 1), (0, -2), (0, -1), (0, 1), (0, 2), (1, -2), (1, -1), (1, 0), (1, 1), (1, 2),)

WIDE = 2
PIECES = HEADS // WIDE

STEPS = (
    (0x403, 0x2301, 0x41B, 0x2311, 0x54B, 0x49, 0x53, 0x114D, 0x59, 0x14, 0x4A, 0x25D, 0x5C, 0xDA, 0xC, 0xC4,),
    (0x50B, 0x114D, 0x413, 0x4A, 0xC, 0x411, 0x443, 0x114, 0x5A, 0x9, 0x5C, 0x341, 0x59, 0x5D, 0xC4, 0xDB,),
    (0x403, 0x54B, 0x1, 0x11, 0x51B, 0x225D, 0x4, 0x53, 0x49, 0x4A, 0x51C, 0x44D, 0x54, 0x59, 0xDA, 0xCC,),
    (0x224D, 0x2C0B, 0x411, 0x59, 0x194A, 0x45D, 0x15A, 0x9, 0x41, 0x2113, 0x5B, 0x15A1C, 0x1D4, 0xC, 0x44, 0xC3,),
    (0x2113, 0x9, 0x45B, 0x19, 0x294A, 0x41, 0x104, 0x1615A, 0x51, 0x4C, 0x40B, 0x14, 0x4D, 0xC3, 0x5C, 0xDD,),
    (0x295A, 0x19, 0x40B, 0x9, 0x51, 0x294A, 0x2143, 0x31C, 0x413, 0xC, 0x5B, 0x44D, 0x54, 0x344, 0xC1, 0xDD,),
    (0x411, 0x401, 0x215A, 0x103, 0x2C59, 0x14, 0x44D, 0x15C, 0x11B, 0x53, 0x304, 0x4DD, 0x49, 0x4B, 0x4C, 0xCA,),
    (0x14A, 0x45D, 0x9, 0x441, 0x11, 0x2103, 0x4D, 0x59, 0xC, 0x4B, 0x13, 0x1C, 0xC4, 0x5B, 0x54, 0xDA,),
    (0x403, 0x413, 0x2311, 0x4B, 0x5B, 0x4, 0x24D, 0x14, 0x4C, 0x1309, 0x5C, 0x441, 0x5D, 0xCA, 0x59, 0xDA,),
    (0x114D, 0x40B, 0x443, 0x115D, 0x1B, 0x104, 0x4C, 0x2C5A, 0x1A19, 0x4A, 0x1C, 0x54, 0x51, 0x9, 0xC1, 0xD3,),
    (0x403, 0x411, 0x413, 0x2209, 0x224D, 0x41, 0x145D, 0x55B, 0x59, 0x4, 0x14, 0x5A, 0xDC, 0x4C, 0x4A, 0xCB,),
    (0x419, 0x224D, 0x25D, 0x209, 0x2C1B, 0x41, 0x403, 0x453, 0x14A, 0x1C, 0x354, 0x4B, 0xC, 0xC4, 0x5A, 0xD1,),
    (0x411, 0x59, 0x104, 0x3, 0x114, 0x9, 0x1B, 0x4A, 0x53, 0x5A, 0x44D, 0x5C, 0x4B, 0xDD, 0x4C, 0xC1,),
    (0x40B, 0x401, 0x41B, 0x49, 0x453, 0x19, 0x4A, 0x45D, 0x1C, 0x30C, 0x4D, 0x144, 0x54, 0x51, 0xDA, 0xC3,),
    (0x401, 0x14A, 0x10B, 0x43, 0x11B, 0x5A, 0x314, 0x4, 0x53, 0x194C, 0xA34D, 0x25C, 0x11, 0x5D, 0xD9, 0xC9,),
    (0x15A, 0x41B, 0x19, 0x4A, 0x153, 0x44D, 0x51, 0xC, 0x9, 0x1C, 0x25D, 0xD4, 0x344, 0xB, 0x41, 0xC3,),
)

FIRST = (
    (0x698,),
    (0x19453,),
    (0x698,),
    (0x116E9,),
    (0x20A,),
    (0x6D9AE9,),
    (0x288,),
    (0x1BAE9,),
    (0x298,),
    (0x964B,),
    (0x298,),
    (0x1366B,),
    (0x688,),
    (0x194E9,),
    (0x298,),
    (0x2B2E9,),
)
FIRST_COUNT = (2, 3, 2, 3, 2, 4, 2, 3, 2, 3, 2, 3, 2, 3, 2, 3)
THEN = (
    (0x192884D1, 0x1B,),
    (0x21B60A, 0x0,),
    (0x25B4E9, 0x0,),
    (0x28B698, 0x0,),
    (0x1B621A4B, 0x0,),
    (0xA688, 0x0,),
    (0x6D9AE9, 0x0,),
    (0x6A0, 0x0,),
    (0x1368965B, 0x2C8,),
    (0x861A, 0x0,),
    (0x136916D9, 0xB,),
    (0x251688, 0x0,),
    (0x66BA5B, 0x0,),
    (0xA2DB698, 0x0,),
    (0x6E926B, 0x0,),
    (0x699898, 0x0,),
)
THEN_COUNT = (6, 4, 4, 4, 5, 3, 4, 2, 7, 3, 6, 4, 4, 5, 4, 4)

SENDS = (18, 15, 13, 22, 17, 18, 18, 10, 17, 17, 18, 18, 10, 15, 17, 13)
FAN = 3

SEEN = {
    0: ((0,), (0, 1)),
    1: ((0, 1), (0, 1)),
    2: ((1,), ()),
    3: ((0,), (0, 1)),
    4: ((0, 1), (0, 1)),
    5: ((1,), ()),
}


def pick(choices, at):
    value = jnp.int32(choices[0])
    for index in range(1, len(choices)):
        value = jnp.where(at == index, choices[index], value)
    return value


def bits(value, low, count):
    return lax.shift_right_logical(value, jnp.int32(low)) & ((1 << count) - 1)


def place(role, piece, block):
    return (role * PIECES + piece) * BLOCKS + block


def kernel(spans_ref, q_ref, k_ref, v_ref, o_ref, order_ref, held, qbuf, obuf, peak, total, acc, hidden,
           send_sem, recv_sem, swap_sem, q_sem, qswap_sem, o_sem, order_sem):
    n_outer = lax.axis_size("outer")
    n_chips = lax.axis_size("inner") // 2
    outer = lax.axis_index("outer")
    inner = lax.axis_index("inner")
    chip, core = inner // 2, inner % 2
    kind = ((outer % 2) * 4 + chip % 4) * 2 + core
    other = 1 - core

    def device(d_outer, d_chip):
        return (
            (outer + d_outer + n_outer) & (n_outer - 1),
            ((chip + d_chip + n_chips) & (n_chips - 1)) * 2 + core,
        )

    twin = (outer, chip * 2 + other)

    barrier = pltpu.get_barrier_semaphore()
    for d_outer, d_chip in OFFSETS:
        pl.semaphore_signal(barrier, 1, device_id=device(-d_outer, -d_chip), device_id_type=MESH)
    pl.semaphore_signal(barrier, 1, device_id=twin, device_id_type=MESH)

    def own_copy(ref, part, head):
        columns = pl.ds((core * HEADS + head) * HEAD, HEAD)
        return pltpu.make_async_copy(
            ref.at[:, columns], held.at[place(0, head // WIDE, core), head % WIDE, part], recv_sem.at[place(0, head // WIDE, core)]
        )

    def twin_copy(ref, part, head):
        columns = pl.ds((other * HEADS + head) * HEAD, HEAD)
        return pltpu.make_async_remote_copy(
            src_ref=ref.at[:, columns],
            dst_ref=held.at[place(0, head // WIDE, core), head % WIDE, part],
            send_sem=swap_sem.at[head, part],
            recv_sem=recv_sem.at[place(0, head // WIDE, core)],
            device_id=twin,
            device_id_type=MESH,
        )

    width = HEADS * QUARTER

    def own_queries():
        return pltpu.make_async_copy(
            q_ref.at[:, pl.ds(core * width, width)], qbuf.at[core], q_sem.at[core]
        )

    def twin_queries():
        return pltpu.make_async_remote_copy(
            src_ref=q_ref.at[:, pl.ds(other * width, width)],
            dst_ref=qbuf.at[core],
            send_sem=qswap_sem,
            recv_sem=q_sem.at[core],
            device_id=twin,
            device_id_type=MESH,
        )

    for head in range(HEADS):
        for part, ref in enumerate((k_ref, v_ref)):
            own_copy(ref, part, head).start()
    own_queries().start()
    spans = pltpu.make_async_copy(spans_ref, order_ref, order_sem)
    spans.start()

    def hidden_tile(role, query_core, key_core):
        d_outer, d_chip = role // 3, role % 3
        at_outer, at_inner = device(-d_outer, -d_chip)
        source = at_outer * (2 * n_chips) + (at_inner - core) + key_core
        mine = outer * (2 * n_chips) + chip * 2 + query_core
        row = lax.broadcasted_iota(jnp.int32, (HEAD, HEAD), 0)
        column = lax.broadcasted_iota(jnp.int32, (HEAD, HEAD), 1)
        half = HEAD // 2
        row_at = jnp.where(row < half, order_ref[2 * mine] * half, order_ref[2 * mine + 1] * half - half) + row
        column_at = (
            jnp.where(column < half, order_ref[2 * source] * half, order_ref[2 * source + 1] * half - half) + column
        )
        return jnp.where(column_at <= row_at, 0.0, MASKED)

    def copy_on(role, block, piece, there):
        far, far_there = (role + 5) >> 3, (there + 5) >> 3
        to = device(far_there - far, (there - 3 * far_there) - (role - 3 * far))
        return pltpu.make_async_remote_copy(
            src_ref=held.at[place(role, piece, block)],
            dst_ref=held.at[place(there, piece, block)],
            send_sem=send_sem,
            recv_sem=recv_sem.at[place(there, piece, block)],
            device_id=to,
            device_id_type=MESH,
        )

    def arrive(slot):
        chunk = held.at[slot]
        pltpu.make_async_copy(chunk, chunk, recv_sem.at[slot]).wait()

    def own_sends(words, count):
        @pl.loop(0, count)
        def _(step):
            code = lax.shift_right_logical(pick(words, lax.div(step, 5)), lax.rem(step, 5) * 6)
            copy_on(0, bits(code, 0, 1), bits(code, 1, 2), bits(code, 3, 3)).start()

    def column(table):
        return [pick([row[at] for row in table], kind) for at in range(len(table[0]))]

    def pass_on(code, role, block, piece, at=0):
        if at == FAN:
            return
        there = bits(code, 8 + 3 * at, 3)

        @pl.when(there > 0)
        def _():
            copy_on(role, block, piece, there).start()
            pass_on(code, role, block, piece, at + 1)

    steps = column(STEPS)
    first, then = column(FIRST), column(THEN)
    first_count, then_count = pick(FIRST_COUNT, kind), pick(THEN_COUNT, kind)
    sends = pick(SENDS, kind)

    pl.semaphore_wait(barrier, len(OFFSETS) + 1)

    for head in range(HEADS):
        for part, ref in enumerate((k_ref, v_ref)):
            twin_copy(ref, part, head).start()

    for piece in range(PIECES):
        arrive(place(0, piece, core))
    own_sends(first, first_count)
    for piece in range(PIECES):
        arrive(place(0, piece, other))
    own_sends(then, then_count)
    twin_queries().start()

    spans.wait()
    for role in range(ROLES):
        for query_core in range(2):
            for key_core in SEEN[role][query_core]:
                hidden[role, query_core, key_core] = hidden_tile(role, query_core, key_core)

    scale = math.log2(math.e) / math.sqrt(HEAD)

    def attend(seen_by, role, piece, wide, fresh=False):
        head = piece * WIDE + wide

        def gather(part, seen):
            return jnp.concatenate([held[place(role, piece, block), wide, part] for block in seen], axis=0)

        for query_core in range(2):
            seen = seen_by[query_core]
            if not seen:
                continue
            queries = jnp.concatenate(
                [
                    qbuf[query_core, :, pl.ds(pl.multiple_of((head * GROUP + at) * HEAD, HEAD), HEAD)]
                    for at in range(GROUP)
                ],
                axis=0,
            )
            score = lax.dot_general(
                queries,
                gather(0, seen),
                (((1,), (1,)), ((), ())),
                preferred_element_type=jnp.float32,
            )
            scores = [
                (
                    score[:, n * HEAD : (n + 1) * HEAD].reshape(GROUP, HEAD, HEAD) * scale
                    + hidden[role, query_core, block][None]
                ).reshape(QUARTER, HEAD)
                for n, block in enumerate(seen)
            ]
            top = scores[0] if len(seen) == 1 else jnp.maximum(scores[0], scores[1])
            top = jnp.broadcast_to(jnp.max(top, axis=1, keepdims=True), (QUARTER, HEAD))
            if not fresh:
                old = peak[query_core, head]
                top = jnp.maximum(old, top)
                factor = jnp.exp2(old - top)
            weights = [jnp.exp2(part - top) for part in scores]
            summed = weights[0] if len(seen) == 1 else weights[0] + weights[1]
            update = jnp.dot(
                jnp.concatenate([weight.astype(jnp.bfloat16) for weight in weights], axis=1),
                gather(1, seen),
                preferred_element_type=jnp.float32,
            )
            if not fresh:
                summed = total[query_core, head] * factor + summed
                update = acc[query_core, head] * factor + update
            peak[query_core, head] = top
            total[query_core, head] = summed
            acc[query_core, head] = update

    for query_core in range(2):
        pltpu.make_async_copy(qbuf.at[query_core], qbuf.at[query_core], q_sem.at[query_core]).wait()

    @pl.loop(0, HEADS)
    def _(head):
        attend(SEEN[0], 0, head // WIDE, head % WIDE, fresh=True)

    def own_result(head):
        columns = pl.ds((core * HEADS + head) * QUARTER, QUARTER)
        return pltpu.make_async_copy(obuf.at[core, head], o_ref.at[:, columns], o_sem.at[0, head])

    def twin_result(head):
        columns = pl.ds((core * HEADS + head) * QUARTER, QUARTER)
        return pltpu.make_async_remote_copy(
            src_ref=obuf.at[other, head],
            dst_ref=o_ref.at[:, columns],
            send_sem=o_sem.at[1, head],
            recv_sem=o_sem.at[2, head],
            device_id=twin,
            device_id_type=MESH,
        )

    def conclude(head):
        for query_core in range(2):
            for at in range(GROUP):
                rows = pl.ds(at * HEAD, HEAD)
                sums = jnp.sum(total[query_core, head, rows], axis=1, keepdims=True)
                result = acc[query_core, head, rows] / sums
                obuf[query_core, head, :, at * HEAD : (at + 1) * HEAD] = result.astype(jnp.bfloat16)
        twin_result(head).start()
        own_result(head).start()

    @pl.loop(0, len(steps))
    def _(step):
        code = pick(steps, step)
        role, block, piece = bits(code, 0, 3), bits(code, 3, 1), bits(code, 4, 2)
        arrive(place(role, piece, block))
        pass_on(code, role, block, piece)
        complete = bits(code, 6, 1)
        for like in (1, 2, 3):
            same = (role == like) | (role == like + 3) if like < 3 else role == 3

            @pl.when((complete == 1) & same)
            def _():
                @pl.loop(0, WIDE)
                def _(wide):
                    attend(SEEN[like], role, piece, wide)

        @pl.when(bits(code, 7, 1) == 1)
        def _():
            @pl.loop(0, WIDE)
            def _(wide):
                conclude(piece * WIDE + wide)

    for head in range(HEADS):
        for part, ref in enumerate((k_ref, v_ref)):
            twin_copy(ref, part, head).wait_send()
    twin_queries().wait_send()
    for count in sorted(set(SENDS)):
        @pl.when(sends == count)
        def _():
            sent = held.at[pl.ds(0, count)]
            pltpu.make_async_copy(sent, sent, send_sem).wait()

    @pl.loop(0, HEADS)
    def _(head):
        own_result(head).wait()
        twin_result(head).wait()


def on_device(queries, keys, values, span_order):
    rows = queries.shape[0]
    return pl.pallas_call(
        kernel,
        out_shape=jax.ShapeDtypeStruct(queries.shape, jnp.bfloat16),
        in_specs=[pl.BlockSpec(memory_space=pltpu.HBM)] * 4,
        out_specs=pl.BlockSpec(memory_space=pl.ANY),
        scratch_shapes=[
            pltpu.SMEM(span_order.shape, jnp.int32),
            pltpu.VMEM((ROLES * PIECES * BLOCKS, WIDE, 2, rows, HEAD), jnp.bfloat16),
            pltpu.VMEM((2, rows, HEADS * QUARTER), jnp.bfloat16),
            pltpu.VMEM((2, HEADS, rows, QUARTER), jnp.bfloat16),
            pltpu.VMEM((2, HEADS, QUARTER, HEAD), jnp.float32),
            pltpu.VMEM((2, HEADS, QUARTER, HEAD), jnp.float32),
            pltpu.VMEM((2, HEADS, QUARTER, HEAD), jnp.float32),
            pltpu.VMEM((ROLES, 2, 2, rows, HEAD), jnp.float32),
            pltpu.SemaphoreType.DMA,
            pltpu.SemaphoreType.DMA((ROLES * PIECES * BLOCKS,)),
            pltpu.SemaphoreType.DMA((HEADS, 2)),
            pltpu.SemaphoreType.DMA((2,)),
            pltpu.SemaphoreType.DMA,
            pltpu.SemaphoreType.DMA((3, HEADS)),
            pltpu.SemaphoreType.DMA,
        ],
        compiler_params=pltpu.CompilerParams(
            collective_id=0, has_side_effects=True, vmem_limit_bytes=52 * 2**20
        ),
        name="attend_window",
    )(*(pltpu.with_memory_space_constraint(one, pltpu.HBM) for one in (span_order, queries, keys, values)))


def solution(mesh):
    rows = P(("outer", "inner"), None)
    return jax.shard_map(
        on_device,
        mesh=mesh,
        in_specs=(rows, rows, rows, P()),
        out_specs=rows,
        check_vma=False,
    )
```

```python
import functools
import math

import jax
import jax.numpy as jnp
from jax import lax
from jax.experimental import pallas as pl
from jax.experimental.pallas import tpu as pltpu
from jax.sharding import PartitionSpec as P

ROLES = 6
BLOCKS = 2
HEADS = 4
GROUP = 4
HEAD = 128
QUARTER = GROUP * HEAD
MESH = pl.DeviceIdType.MESH
MASKED = -1e30

OFFSETS = ((-1, -1), (-1, 0), (-1, 1), (0, -2), (0, -1), (0, 1), (0, 2), (1, -2), (1, -1), (1, 0), (1, 1), (1, 2),)

WIDE = 2
PIECES = HEADS // WIDE

STEPS = (
    (0x403, 0x2301, 0x41B, 0x2311, 0x54B, 0x49, 0x53, 0x114D, 0x59, 0x14, 0x25D, 0x4A, 0x5C, 0xDA, 0xC, 0xC4,),
    (0x50B, 0x114D, 0x413, 0x4A, 0xC, 0x114, 0x443, 0x411, 0x5A, 0x5C, 0x301, 0x49, 0x59, 0x5D, 0xC4, 0xDB,),
    (0x403, 0x54B, 0x51B, 0x1, 0x11, 0x49, 0x4A, 0x4, 0x53, 0x225D, 0x51C, 0x44D, 0x54, 0x59, 0xCC, 0xDA,),
    (0x224D, 0x2C0B, 0x411, 0x59, 0x45D, 0x194A, 0x15A, 0x1, 0x2113, 0x49, 0x15A1C, 0x154, 0xDB, 0x4, 0x4C, 0xC3,),
    (0x2113, 0x9, 0x45B, 0x294A, 0x19, 0x104, 0x1615A, 0x41, 0x51, 0x4C, 0x40B, 0x14, 0x4D, 0x5C, 0xDD, 0xC3,),
    (0x295A, 0x19, 0x40B, 0x51, 0x9, 0x294A, 0x2143, 0x413, 0x31C, 0xC, 0x44D, 0x5B, 0x54, 0x344, 0xDD, 0xC1,),
    (0x411, 0x401, 0x215A, 0x103, 0x2C59, 0x14, 0x44D, 0x15C, 0x11B, 0x45D, 0xD3, 0x4A, 0x304, 0x49, 0x4B, 0xCC,),
    (0x14A, 0x45D, 0x401, 0x49, 0x2103, 0x11, 0x4D, 0xC, 0x4B, 0x59, 0x13, 0xC4, 0x1C, 0x54, 0x5B, 0xDA,),
    (0x403, 0x413, 0x2311, 0x4B, 0x5B, 0x4, 0x4C, 0x24D, 0x14, 0x1309, 0x5C, 0x441, 0x5D, 0x59, 0xCA, 0xDA,),
    (0x114D, 0x40B, 0x443, 0x115D, 0x1B, 0x104, 0x2C5A, 0x4C, 0x1A19, 0x4A, 0x1C, 0x51, 0x54, 0x9, 0xC1, 0xD3,),
    (0x403, 0x411, 0x413, 0x2209, 0x224D, 0x41, 0x145D, 0x55B, 0x59, 0x4, 0x14, 0x4C, 0x4B, 0x5C, 0xCA, 0xDA,),
    (0x419, 0x224D, 0x25D, 0x209, 0x2C1B, 0x41, 0x403, 0x453, 0x14A, 0x314, 0x5C, 0xC, 0x4B, 0xC4, 0x5A, 0xD1,),
    (0x411, 0x59, 0x3, 0x104, 0x1B, 0x114, 0x9, 0x4A, 0x5A, 0x44D, 0x5C, 0x53, 0x4C, 0xDD, 0x4B, 0xC1,),
    (0x40B, 0x401, 0x41B, 0x49, 0x453, 0x19, 0x45D, 0x30C, 0x4A, 0x4D, 0x1C, 0x144, 0x54, 0x51, 0xC3, 0xDA,),
    (0x401, 0x14A, 0x10B, 0x5A, 0x11B, 0x43, 0x314, 0xA34D, 0x190C, 0x44, 0x53, 0x25C, 0x11, 0x59, 0xDD, 0xC9,),
    (0x15A, 0x41B, 0x19, 0x4A, 0x153, 0x44D, 0x51, 0x9, 0xC, 0x1C, 0x25D, 0x344, 0xD4, 0xB, 0x41, 0xC3,),
)

FIRST = (
    (0x698,),
    (0x19453,),
    (0x698,),
    (0x116E9,),
    (0x20A,),
    (0x6D9AE9,),
    (0x288,),
    (0x1BAE9,),
    (0x298,),
    (0x964B,),
    (0x298,),
    (0x1366B,),
    (0x688,),
    (0x194E9,),
    (0x298,),
    (0x2B2E9,),
)
FIRST_COUNT = (2, 3, 2, 3, 2, 4, 2, 3, 2, 3, 2, 3, 2, 3, 2, 3)
THEN = (
    (0x192884D1, 0x1B,),
    (0x21B60A, 0x0,),
    (0x25B4E9, 0x0,),
    (0x28B698, 0x0,),
    (0x1B621A4B, 0x0,),
    (0xA688, 0x0,),
    (0x6D9AE9, 0x0,),
    (0x6A0, 0x0,),
    (0x1368965B, 0x2C8,),
    (0x861A, 0x0,),
    (0x136916D9, 0xB,),
    (0x251688, 0x0,),
    (0x66BA5B, 0x0,),
    (0xA2DB698, 0x0,),
    (0x6E926B, 0x0,),
    (0x699898, 0x0,),
)
THEN_COUNT = (6, 4, 4, 4, 5, 3, 4, 2, 7, 3, 6, 4, 4, 5, 4, 4)

SENDS = (18, 15, 13, 22, 17, 18, 18, 10, 17, 17, 18, 18, 10, 15, 17, 13)
FAN = 3

SEEN = {
    0: ((0,), (0, 1)),
    1: ((0, 1), (0, 1)),
    2: ((1,), ()),
    3: ((0,), (0, 1)),
    4: ((0, 1), (0, 1)),
    5: ((1,), ()),
}


def pick(choices, at):
    value = jnp.int32(choices[0])
    for index in range(1, len(choices)):
        value = jnp.where(at == index, choices[index], value)
    return value


def bits(value, low, count):
    return lax.shift_right_logical(value, jnp.int32(low)) & ((1 << count) - 1)


def place(role, piece, block):
    return (role * PIECES + piece) * BLOCKS + block


def kernel(spans_ref, q_ref, k_ref, v_ref, o_ref, order_ref, held, qbuf, obuf, peak, total, acc, hidden,
           send_sem, recv_sem, swap_sem, q_sem, qswap_sem, o_sem, order_sem):
    n_outer = lax.axis_size("outer")
    n_chips = lax.axis_size("inner") // 2
    outer = lax.axis_index("outer")
    inner = lax.axis_index("inner")
    chip, core = inner // 2, inner % 2
    kind = ((outer % 2) * 4 + chip % 4) * 2 + core
    other = 1 - core

    def device(d_outer, d_chip):
        return (
            (outer + d_outer + n_outer) & (n_outer - 1),
            ((chip + d_chip + n_chips) & (n_chips - 1)) * 2 + core,
        )

    twin = (outer, chip * 2 + other)

    barrier = pltpu.get_barrier_semaphore()
    for d_outer, d_chip in OFFSETS:
        pl.semaphore_signal(barrier, 1, device_id=device(-d_outer, -d_chip), device_id_type=MESH)
    pl.semaphore_signal(barrier, 1, device_id=twin, device_id_type=MESH)

    def own_copy(ref, part, head):
        columns = pl.ds((core * HEADS + head) * HEAD, HEAD)
        return pltpu.make_async_copy(
            ref.at[:, columns], held.at[place(0, head // WIDE, core), head % WIDE, part], recv_sem.at[place(0, head // WIDE, core)]
        )

    def twin_copy(ref, part, head):
        columns = pl.ds((other * HEADS + head) * HEAD, HEAD)
        return pltpu.make_async_remote_copy(
            src_ref=ref.at[:, columns],
            dst_ref=held.at[place(0, head // WIDE, core), head % WIDE, part],
            send_sem=swap_sem.at[head, part],
            recv_sem=recv_sem.at[place(0, head // WIDE, core)],
            device_id=twin,
            device_id_type=MESH,
        )

    width = HEADS * QUARTER

    def own_queries():
        return pltpu.make_async_copy(
            q_ref.at[:, pl.ds(core * width, width)], qbuf.at[core], q_sem.at[core]
        )

    def twin_queries():
        return pltpu.make_async_remote_copy(
            src_ref=q_ref.at[:, pl.ds(other * width, width)],
            dst_ref=qbuf.at[core],
            send_sem=qswap_sem,
            recv_sem=q_sem.at[core],
            device_id=twin,
            device_id_type=MESH,
        )

    for head in range(HEADS):
        for part, ref in enumerate((k_ref, v_ref)):
            own_copy(ref, part, head).start()
    own_queries().start()
    spans = pltpu.make_async_copy(spans_ref, order_ref, order_sem)
    spans.start()

    def hidden_tile(role, query_core, key_core):
        d_outer, d_chip = role // 3, role % 3
        at_outer, at_inner = device(-d_outer, -d_chip)
        source = at_outer * (2 * n_chips) + (at_inner - core) + key_core
        mine = outer * (2 * n_chips) + chip * 2 + query_core
        row = lax.broadcasted_iota(jnp.int32, (HEAD, HEAD), 0)
        column = lax.broadcasted_iota(jnp.int32, (HEAD, HEAD), 1)
        half = HEAD // 2
        row_at = jnp.where(row < half, order_ref[2 * mine] * half, order_ref[2 * mine + 1] * half - half) + row
        column_at = (
            jnp.where(column < half, order_ref[2 * source] * half, order_ref[2 * source + 1] * half - half) + column
        )
        return jnp.where(column_at <= row_at, 0.0, MASKED)

    def copy_on(role, block, piece, there):
        far, far_there = (role + 5) >> 3, (there + 5) >> 3
        to = device(far_there - far, (there - 3 * far_there) - (role - 3 * far))
        return pltpu.make_async_remote_copy(
            src_ref=held.at[place(role, piece, block)],
            dst_ref=held.at[place(there, piece, block)],
            send_sem=send_sem,
            recv_sem=recv_sem.at[place(there, piece, block)],
            device_id=to,
            device_id_type=MESH,
        )

    def arrive(slot):
        chunk = held.at[slot]
        pltpu.make_async_copy(chunk, chunk, recv_sem.at[slot]).wait()

    def own_sends(words, count):
        @pl.loop(0, count)
        def _(step):
            code = lax.shift_right_logical(pick(words, lax.div(step, 5)), lax.rem(step, 5) * 6)
            copy_on(0, bits(code, 0, 1), bits(code, 1, 2), bits(code, 3, 3)).start()

    def column(table):
        return [pick([row[at] for row in table], kind) for at in range(len(table[0]))]

    def pass_on(code, role, block, piece, at=0):
        if at == FAN:
            return
        there = bits(code, 8 + 3 * at, 3)

        @pl.when(there > 0)
        def _():
            copy_on(role, block, piece, there).start()
            pass_on(code, role, block, piece, at + 1)

    steps = column(STEPS)
    first, then = column(FIRST), column(THEN)
    first_count, then_count = pick(FIRST_COUNT, kind), pick(THEN_COUNT, kind)
    sends = pick(SENDS, kind)

    pl.semaphore_wait(barrier, len(OFFSETS) + 1)

    for head in range(HEADS):
        for part, ref in enumerate((k_ref, v_ref)):
            twin_copy(ref, part, head).start()

    for piece in range(PIECES):
        arrive(place(0, piece, core))
    own_sends(first, first_count)
    for piece in range(PIECES):
        arrive(place(0, piece, other))
    own_sends(then, then_count)
    twin_queries().start()

    spans.wait()
    for role in range(ROLES):
        for query_core in range(2):
            for key_core in SEEN[role][query_core]:
                hidden[role, query_core, key_core] = hidden_tile(role, query_core, key_core)

    scale = math.log2(math.e) / math.sqrt(HEAD)

    def attend(seen_by, role, piece, wide, fresh=False):
        head = piece * WIDE + wide

        def gather(part, seen):
            return jnp.concatenate([held[place(role, piece, block), wide, part] for block in seen], axis=0)

        for query_core in range(2):
            seen = seen_by[query_core]
            if not seen:
                continue
            queries = jnp.concatenate(
                [
                    qbuf[query_core, :, pl.ds(pl.multiple_of((head * GROUP + at) * HEAD, HEAD), HEAD)]
                    for at in range(GROUP)
                ],
                axis=0,
            )
            score = lax.dot_general(
                queries,
                gather(0, seen),
                (((1,), (1,)), ((), ())),
                preferred_element_type=jnp.float32,
            )
            scores = [
                (
                    score[:, n * HEAD : (n + 1) * HEAD].reshape(GROUP, HEAD, HEAD) * scale
                    + hidden[role, query_core, block][None]
                ).reshape(QUARTER, HEAD)
                for n, block in enumerate(seen)
            ]
            top = scores[0] if len(seen) == 1 else jnp.maximum(scores[0], scores[1])
            top = jnp.broadcast_to(jnp.max(top, axis=1, keepdims=True), (QUARTER, HEAD))
            if not fresh:
                old = peak[query_core, head]
                top = jnp.maximum(old, top)
                factor = jnp.exp2(old - top)
            weights = [jnp.exp2(part - top) for part in scores]
            summed = weights[0] if len(seen) == 1 else weights[0] + weights[1]
            update = jnp.dot(
                jnp.concatenate([weight.astype(jnp.bfloat16) for weight in weights], axis=1),
                gather(1, seen),
                preferred_element_type=jnp.float32,
            )
            if not fresh:
                summed = total[query_core, head] * factor + summed
                update = acc[query_core, head] * factor + update
            peak[query_core, head] = top
            total[query_core, head] = summed
            acc[query_core, head] = update

    for query_core in range(2):
        pltpu.make_async_copy(qbuf.at[query_core], qbuf.at[query_core], q_sem.at[query_core]).wait()

    @pl.loop(0, HEADS)
    def _(head):
        attend(SEEN[0], 0, head // WIDE, head % WIDE, fresh=True)

    def own_result(head):
        columns = pl.ds((core * HEADS + head) * QUARTER, QUARTER)
        return pltpu.make_async_copy(obuf.at[core, head], o_ref.at[:, columns], o_sem.at[0, head])

    def twin_result(head):
        columns = pl.ds((core * HEADS + head) * QUARTER, QUARTER)
        return pltpu.make_async_remote_copy(
            src_ref=obuf.at[other, head],
            dst_ref=o_ref.at[:, columns],
            send_sem=o_sem.at[1, head],
            recv_sem=o_sem.at[2, head],
            device_id=twin,
            device_id_type=MESH,
        )

    def conclude(head):
        for query_core in range(2):
            for at in range(GROUP):
                rows = pl.ds(at * HEAD, HEAD)
                sums = jnp.sum(total[query_core, head, rows], axis=1, keepdims=True)
                result = acc[query_core, head, rows] / sums
                obuf[query_core, head, :, at * HEAD : (at + 1) * HEAD] = result.astype(jnp.bfloat16)
        twin_result(head).start()
        own_result(head).start()

    @pl.loop(0, len(steps))
    def _(step):
        code = pick(steps, step)
        role, block, piece = bits(code, 0, 3), bits(code, 3, 1), bits(code, 4, 2)
        arrive(place(role, piece, block))
        pass_on(code, role, block, piece)
        complete = bits(code, 6, 1)
        for like in (1, 2, 3):
            same = (role == like) | (role == like + 3) if like < 3 else role == 3

            @pl.when((complete == 1) & same)
            def _():
                @pl.loop(0, WIDE)
                def _(wide):
                    attend(SEEN[like], role, piece, wide)

        @pl.when(bits(code, 7, 1) == 1)
        def _():
            @pl.loop(0, WIDE)
            def _(wide):
                conclude(piece * WIDE + wide)

    for head in range(HEADS):
        for part, ref in enumerate((k_ref, v_ref)):
            twin_copy(ref, part, head).wait_send()
    twin_queries().wait_send()
    for count in sorted(set(SENDS)):
        @pl.when(sends == count)
        def _():
            sent = held.at[pl.ds(0, count)]
            pltpu.make_async_copy(sent, sent, send_sem).wait()

    @pl.loop(0, HEADS)
    def _(head):
        own_result(head).wait()
        twin_result(head).wait()


def on_device(queries, keys, values, span_order):
    rows = queries.shape[0]
    return pl.pallas_call(
        kernel,
        out_shape=jax.ShapeDtypeStruct(queries.shape, jnp.bfloat16),
        in_specs=[pl.BlockSpec(memory_space=pltpu.HBM)] * 4,
        out_specs=pl.BlockSpec(memory_space=pl.ANY),
        scratch_shapes=[
            pltpu.SMEM(span_order.shape, jnp.int32),
            pltpu.VMEM((ROLES * PIECES * BLOCKS, WIDE, 2, rows, HEAD), jnp.bfloat16),
            pltpu.VMEM((2, rows, HEADS * QUARTER), jnp.bfloat16),
            pltpu.VMEM((2, HEADS, rows, QUARTER), jnp.bfloat16),
            pltpu.VMEM((2, HEADS, QUARTER, HEAD), jnp.float32),
            pltpu.VMEM((2, HEADS, QUARTER, HEAD), jnp.float32),
            pltpu.VMEM((2, HEADS, QUARTER, HEAD), jnp.float32),
            pltpu.VMEM((ROLES, 2, 2, rows, HEAD), jnp.float32),
            pltpu.SemaphoreType.DMA,
            pltpu.SemaphoreType.DMA((ROLES * PIECES * BLOCKS,)),
            pltpu.SemaphoreType.DMA((HEADS, 2)),
            pltpu.SemaphoreType.DMA((2,)),
            pltpu.SemaphoreType.DMA,
            pltpu.SemaphoreType.DMA((3, HEADS)),
            pltpu.SemaphoreType.DMA,
        ],
        compiler_params=pltpu.CompilerParams(
            collective_id=0, has_side_effects=True, vmem_limit_bytes=52 * 2**20
        ),
        name="attend_window",
    )(*(pltpu.with_memory_space_constraint(one, pltpu.HBM) for one in (span_order, queries, keys, values)))


def solution(mesh):
    rows = P(("outer", "inner"), None)
    return jax.shard_map(
        on_device,
        mesh=mesh,
        in_specs=(rows, rows, rows, P()),
        out_specs=rows,
        check_vma=False,
    )
```
